32 devices in a mesh: plans: 2 (over y), vox: 8 (over z, x), beam: 2 (over core).
Axes of the slice: x: 2, y: 2, z: 4, core: 2. Of those that a mesh axis runs over, the one named last changes fastest.
Arguments:
- fluence: float32 [16, 2, 16384], P('plans', 'beam', 'vox'), parts along dimension 0, may hold values from 0 to 1
- tile_values: float32 [16, 2, 32, 128, 128], P(('plans', 'vox'), 'beam'), parts along dimension 0, may hold values from 0 to 0.015625
- tile_rows: int32 [16, 2, 32], P(('plans', 'vox'), 'beam'), parts along dimension 0, may hold values from 0 to 31, as said below
- tile_columns: int32 [16, 2, 32], P(('plans', 'vox'), 'beam'), parts along dimension 0, may hold values from 0 to 127, as said below
- tile_count: int32 [16, 2], P(('plans', 'vox'), 'beam'), parts along dimension 0, may hold values from 1 to 32, as said below
- labels: int32 [65536], P(('plans', 'vox')), parts along dimension 0, may hold values from 0 to 3
- prescribed: float32 [8], P('plans'), parts along dimension 0, may hold values from 0.2 to 1
- weights: float32 [16, 4], P('plans'), parts along dimension 0, may hold values from 0.5 to 4
- smoothing: float32 [16], P('plans'), parts along dimension 0, may hold values from 0.2 to 2
- beam_neighbours: int32 [128, 3], P('plans'), parts along dimension 0, may hold values from 0 to 63, as said below
Outputs:
- dose_field: float32 [16, 32768], P('plans', 'vox'), parts along dimension 0
- gradient: float32 [16, 2, 16384], P('plans', 'beam', 'vox'), parts along dimension 0
The draws below stay inside these ranges and needn't reach their ends.
There are 2 independent parts, one for each index of `plans`. The reference program is written for one: setup_inputs(seed, part) draws one part's arguments, and reference() takes and returns one part's arrays. A program takes and returns all parts, laid end to end along the dimension named above; each array names one. Nothing has to cross between parts.
Inputs may be any that keep to these rules, and one draw needn't show every extreme that they name: The pairs (tile_rows, tile_columns) of one device's 32 slots are distinct; entries of slots at or after that device's tile_count are ignored. `tile_columns`: see tile_rows. `tile_count`: uneven over devices; some device uses all 32 slots. `beam_neighbours`: every beam appears as some beam's neighbour.
All inputs are finite; a program needn't handle non-finite values.
Results may differ from the reference program's by a relative error of at most 0.0003.
Values sent between devices are 32-bit elements; how exact they have to be, the bound alone decides.
A program may use at most 64 MiB of HBM per device.

```python
import math
import jax
import jax.numpy as jnp
from jax import lax

TILE = 128
BLB = 512
NSTRUCT = 4
K = 8
RB_DEV = 32
CBB = 128
CAP = 32
NVOX = 32768
GBL = 16384
NBEAMS = 64
N_VOX = 8
N_BEAM = 2


def tile_cells(key):
    device_keys = jax.random.split(key, N_VOX * N_BEAM)

    def one_device(device_key):
        return jax.random.permutation(device_key, RB_DEV * CBB)[:CAP]
    cells = jax.vmap(one_device)(device_keys)
    return cells.reshape(N_VOX, N_BEAM, CAP).astype(jnp.int32)


def draw_tile_rows(key, part):
    cells = tile_cells(key)
    return (cells // CBB).astype(jnp.int32)


def draw_tile_columns(key, part):
    cells = tile_cells(key)
    return (cells % CBB).astype(jnp.int32)


def draw_tile_count(key, part):
    key = jax.random.fold_in(key, 7)
    first_key, second_key, third_key = jax.random.split(key, 3)
    first = jax.random.randint(first_key, (N_VOX * N_BEAM,), 0, CAP + 1)
    second = jax.random.randint(second_key, (N_VOX * N_BEAM,), 0, CAP + 1)
    counts = jnp.maximum(first * second // CAP, 1)
    chosen = jax.random.randint(third_key, (), 0, N_VOX * N_BEAM)
    counts = jnp.where(jnp.arange(N_VOX * N_BEAM) == chosen, CAP, counts)
    return counts.reshape(N_VOX, N_BEAM).astype(jnp.int32)


def draw_beam_neighbours(key, part):
    key = jax.random.fold_in(key, 11)
    layout = jax.random.permutation(key, NBEAMS).astype(jnp.int32)
    where_is = jnp.argsort(layout).astype(jnp.int32)
    cycle = NBEAMS // 2
    couch_row = where_is // cycle
    gantry = where_is % cycle
    before = layout[couch_row * cycle + (gantry + cycle - 1) % cycle]
    after = layout[couch_row * cycle + (gantry + 1) % cycle]
    across = layout[(1 - couch_row) * cycle + gantry]
    return jnp.stack([before, after, across], axis=1).astype(jnp.int32)


def plant(values, own_key, low, high):
    shape = values.shape
    spot = [jax.random.randint(jax.random.fold_in(own_key, axis), (), 0, shape[axis]) for axis in range(len(shape))]
    values = values.at[tuple(spot)].set(low)
    longest = shape.index(max(shape))
    spot[longest] = (spot[longest] + 1) % shape[longest]
    return values.at[tuple(spot)].set(high)


def shard_levels(own_key, extent, shards, smallest, top_value):
    gain, own = 1.0, jax.random.fold_in(own_key, 6)
    for position, blocks in shards:
        steps = jnp.exp(jax.random.uniform(jax.random.fold_in(own, position), (blocks,), jnp.float32, smallest / len(shards), top_value / len(shards)))
        gain = gain * jnp.repeat(steps, extent[position] // blocks).reshape([-1 if axis == position else 1 for axis in range(len(extent))])
    return gain


def setup_inputs(seed: int = 0, part: int = 0) -> dict:
    key_of = jax.random.split(jax.random.key(seed), 11)
    own_keys = jax.random.split(jax.random.fold_in(key_of[10], part), 11)
    return {
        "fluence": jnp.clip(1.0 * jax.random.uniform(own_keys[0], (K, N_BEAM, GBL), jnp.float32) ** shard_levels(own_keys[0], (K, N_BEAM, GBL), ((1, 2), (2, 8)), -0.2, 0.2), 0.0, 1.0),
        "tile_values": jnp.clip(0.015625 * jax.random.uniform(own_keys[1], (N_VOX, N_BEAM, CAP, TILE, TILE), jnp.float32) ** shard_levels(own_keys[1], (N_VOX, N_BEAM, CAP, TILE, TILE), ((0, 8), (1, 2)), -0.2, 0.2), 0.0, 0.015625),
        "tile_rows": draw_tile_rows(jax.random.fold_in(jax.random.fold_in(key_of[10], part), 71), part),
        "tile_columns": draw_tile_columns(jax.random.fold_in(jax.random.fold_in(key_of[10], part), 71), part),
        "tile_count": draw_tile_count(jax.random.fold_in(jax.random.fold_in(key_of[10], part), 71), part),
        "labels": plant(jax.random.randint(own_keys[5], (NVOX,), 0, NSTRUCT), jax.random.fold_in(own_keys[5], 1), 0, NSTRUCT - 1).astype(jnp.int32),
        "prescribed": jnp.clip(jax.random.uniform(own_keys[6], (NSTRUCT,), jnp.float32, 0.2, 1.0), 0.2, 1.0),
        "weights": jnp.clip(jnp.exp(jax.random.uniform(own_keys[7], (K, NSTRUCT), jnp.float32, math.log(0.5), math.log(4.0))), 0.5, 4.0),
        "smoothing": jnp.clip(jnp.exp(jax.random.uniform(own_keys[8], (K,), jnp.float32, math.log(0.2), math.log(2.0))), 0.2, 2.0),
        "beam_neighbours": draw_beam_neighbours(jax.random.fold_in(jax.random.fold_in(key_of[10], part), 71), part),
    }


highest = lax.Precision.HIGHEST


def penalty_residual(dose, labels, prescribed, weights):
    target = jnp.zeros(dose.shape[1:], jnp.float32)
    scaled = jnp.zeros(dose.shape, jnp.float32)
    for structure in range(prescribed.shape[0]):
        member = labels == structure
        target = jnp.where(member, prescribed[structure], target)
        scaled = jnp.where(member[None, :], weights[:, structure:structure + 1], scaled)
    excess = dose - target[None, :]
    excess = jnp.where(labels[None, :] == 0, excess, jnp.maximum(excess, 0.0))
    return scaled * excess


def reference(fluence, tile_values, tile_rows, tile_columns, tile_count, labels, prescribed, weights, smoothing, beam_neighbours):
    blocks = fluence.reshape(K, N_BEAM, CBB, TILE)
    slots = jnp.arange(CAP)

    def dose_of(index):
        total = jnp.zeros((K, RB_DEV, TILE), jnp.float32)
        for group in range(N_BEAM):
            values = tile_values[index, group]
            row_list = tile_rows[index, group]
            column_list = tile_columns[index, group]
            active = slots < tile_count[index, group]
            picked = jnp.take(blocks[:, group], column_list, axis=1)
            product = jnp.einsum("kst,sut->ksu", picked, values, precision=highest)
            place = jnp.where((row_list[None, :] == jnp.arange(RB_DEV)[:, None]) & active[None, :], 1.0, 0.0).astype(jnp.float32)
            total = total + jnp.einsum("rs,ksu->kru", place, product, precision=highest)
        return total

    dose_blocks = lax.map(dose_of, jnp.arange(N_VOX))
    dose_field = jnp.transpose(dose_blocks, (1, 0, 2, 3)).reshape(K, NVOX)
    residual = penalty_residual(dose_field, labels, prescribed, weights)
    residual_blocks = residual.reshape(K, N_VOX, RB_DEV, TILE)

    def add_device(carry, index):
        here = lax.dynamic_index_in_dim(residual_blocks, index, 1, keepdims=False)
        terms = []
        for group in range(N_BEAM):
            values = tile_values[index, group]
            row_list = tile_rows[index, group]
            column_list = tile_columns[index, group]
            active = slots < tile_count[index, group]
            picked = jnp.take(here, row_list, axis=1)
            product = jnp.einsum("ksu,sut->kst", picked, values, precision=highest)
            place = jnp.where((column_list[None, :] == jnp.arange(CBB)[:, None]) & active[None, :], 1.0, 0.0).astype(jnp.float32)
            terms.append(jnp.einsum("cs,kst->kct", place, product, precision=highest))
        return carry + jnp.stack(terms, axis=1), None

    adjoint, _ = lax.scan(add_device, jnp.zeros((K, N_BEAM, CBB, TILE), jnp.float32), jnp.arange(N_VOX))
    whole = fluence.reshape(K, NBEAMS, BLB)
    beside_all = jnp.zeros_like(whole)
    for neighbour in range(beam_neighbours.shape[1]):
        beside_all = beside_all + jnp.take(whole, beam_neighbours[:, neighbour], axis=1)
    spread = beam_neighbours.shape[1] * whole - beside_all
    gradient = adjoint.reshape(K, N_BEAM, GBL) + smoothing[:, None, None] * spread.reshape(K, N_BEAM, GBL)
    return dose_field, gradient
```

```python
import functools

import jax
import jax.numpy as jnp
from jax import lax
from jax.experimental import pallas as pl
from jax.experimental.pallas import tpu as pltpu
from jax.sharding import PartitionSpec as P

TILE = 128
BLB = 512
MESH = pl.DeviceIdType.MESH
F32 = jnp.float32
BF16 = jnp.bfloat16


def two_terms(x):
    high = x.astype(BF16)
    return high, (x - high.astype(F32)).astype(BF16)


def three_terms(x):
    high = x.astype(BF16)
    rest = x - high.astype(F32)
    middle = rest.astype(BF16)
    return high, middle, (rest - middle.astype(F32)).astype(BF16)


def dot(a, b, on=0):
    return lax.dot_general(a, b, (((1,), (on,)), ((), ())), preferred_element_type=F32)


def kernel(
    parts,
    groups,
    fluence,
    values,
    row_list,
    column_list,
    row_vector,
    column_vector,
    count,
    labels,
    prescribed,
    weights,
    smoothing,
    neighbours,
    dose_out,
    gradient_out,
    tiles,
    split,
    own,
    other,
    product,
    partial,
    partner_partial,
    residual,
    terms,
    arrived,
    base,
    load_sem,
    gather_send,
    gather_recv,
    pair_send,
    pair_recv,
    scatter_send,
    scatter_recv,
):
    me = lax.axis_index("vox")
    group = lax.axis_index("beam")
    partner = lax.rem(group + 1, groups)
    k_count = fluence.shape[0]
    blocks_here = fluence.shape[2] // TILE
    row_blocks = labels.shape[0]
    slots = tiles.shape[0]
    column_blocks = own.shape[0]
    chunks = load_sem.shape[0]
    chunk = slots // chunks
    peers = [lax.rem(me + step, parts) for step in range(1, parts)]

    loads = []
    for part in range(chunks):
        here = pl.ds(part * chunk, chunk)
        copy = pltpu.make_async_copy(values.at[0, 0, here], tiles.at[here], load_sem.at[part])
        copy.start()
        loads.append(copy)

    barrier = pltpu.get_barrier_semaphore()
    for peer in peers:
        pl.semaphore_signal(barrier, inc=1, device_id={"vox": peer}, device_id_type=MESH)
    pl.semaphore_signal(barrier, inc=1, device_id={"beam": partner}, device_id_type=MESH)

    for block in range(blocks_here):
        own[me * blocks_here + block] = fluence[:, 0, block * TILE : (block + 1) * TILE]

    pl.semaphore_wait(barrier, parts)

    mine = pl.ds(me * blocks_here, blocks_here)
    gathers = []
    for step, peer in enumerate(peers):
        copy = pltpu.make_async_remote_copy(
            src_ref=own.at[mine],
            dst_ref=own.at[mine],
            send_sem=gather_send.at[step],
            recv_sem=gather_recv.at[step],
            device_id={"vox": peer},
            device_id_type=MESH,
        )
        copy.start()
        gathers.append(copy)

    for part in range(chunks):
        loads[part].wait()
        for slot in range(part * chunk, (part + 1) * chunk):
            high, low = two_terms(tiles[slot])
            split[slot, :TILE] = high
            split[slot, TILE:] = low

    for copy in gathers:
        copy.wait_recv()

    share = pltpu.make_async_remote_copy(
        src_ref=own,
        dst_ref=other,
        send_sem=pair_send.at[0],
        recv_sem=pair_recv.at[0],
        device_id={"beam": partner},
        device_id_type=MESH,
    )
    share.start()

    for slot in range(slots):
        high, low = two_terms(own[column_list[0, 0, slot]])
        out = dot(jnp.concatenate([high, low], axis=0), split[slot], on=1)
        out = out[:k_count] + out[k_count:]
        product[pl.ds(slot, k_count, stride=slots), :] = out[:, :TILE] + out[:, TILE:]

    active = lax.broadcasted_iota(jnp.int32, (1, slots), 1) < count[0, 0]

    def placed(vector, length):
        blocks = lax.broadcasted_iota(jnp.int32, (length, slots), 0)
        place = jnp.where((vector == blocks) & active, 1.0, 0.0).astype(BF16)
        wide = jnp.concatenate(
            [product[k * slots : (k + 1) * slots, :] for k in range(k_count)], axis=1
        )
        high, middle, low = three_terms(wide)
        return dot(place, high) + (dot(place, middle) + dot(place, low))

    dose = placed(row_vector[0], row_blocks)
    for k in range(k_count):
        partial[k * row_blocks : (k + 1) * row_blocks, :] = dose[:, k * TILE : (k + 1) * TILE]
    swap = pltpu.make_async_remote_copy(
        src_ref=partial,
        dst_ref=partner_partial,
        send_sem=pair_send.at[1],
        recv_sem=pair_recv.at[1],
        device_id={"beam": partner},
        device_id_type=MESH,
    )
    swap.start()

    k_index = lax.broadcasted_iota(jnp.int32, (k_count, TILE), 0)

    def spread_over_k(read):
        column = jnp.zeros((k_count, TILE), F32)
        for k in range(k_count):
            column = jnp.where(k_index == k, read(k), column)
        return column

    weight_of = [
        spread_over_k(lambda k, s=s: weights[k, s]) for s in range(prescribed.shape[0])
    ]
    smooth = spread_over_k(lambda k: smoothing[k])

    swap.wait_recv()
    for row in range(row_blocks):
        where = pl.ds(row, k_count, stride=row_blocks)
        total = partial[where, :] + partner_partial[where, :]
        dose_out[:, row * TILE : (row + 1) * TILE] = total
        label = jnp.broadcast_to(labels[row : row + 1, :], (k_count, TILE))
        target = jnp.zeros((k_count, TILE), F32)
        scaled = jnp.zeros((k_count, TILE), F32)
        for structure in range(prescribed.shape[0]):
            member = label == structure
            target = jnp.where(member, prescribed[structure], target)
            scaled = jnp.where(member, weight_of[structure], scaled)
        excess = total - target
        excess = jnp.where(label == 0, excess, jnp.maximum(excess, 0.0))
        residual[row] = scaled * excess

    for slot in range(slots):
        high, low = two_terms(residual[row_list[0, 0, slot]])
        both = jnp.concatenate([high, low], axis=0)
        out = dot(jnp.concatenate([both, both], axis=1), split[slot])
        product[pl.ds(slot, k_count, stride=slots), :] = out[:k_count] + out[k_count:]

    adjoint = placed(column_vector[0], column_blocks)
    for part in range(parts):
        terms[part] = adjoint[part * blocks_here : (part + 1) * blocks_here, :]
    scatters = []
    for step, peer in enumerate(peers):
        copy = pltpu.make_async_remote_copy(
            src_ref=terms.at[peer],
            dst_ref=arrived.at[step],
            send_sem=scatter_send.at[step],
            recv_sem=scatter_recv.at[step],
            device_id={"vox": peer},
            device_id_type=MESH,
        )
        copy.start()
        scatters.append(copy)

    share.wait_recv()
    per_beam = BLB // TILE
    group_beams = column_blocks // per_beam
    near = neighbours.shape[1]
    for block in range(blocks_here):
        place = group * column_blocks + me * blocks_here + block
        beam = place // per_beam
        within = place % per_beam
        around = jnp.zeros((k_count, TILE), F32)
        for n in range(near):
            beside = neighbours[beam, n]
            in_other = jnp.where(beside >= group_beams, 1, 0)
            at = (beside - in_other * group_beams) * per_beam + within
            around = around + jnp.where(in_other == group, own[at], other[at])
        here = fluence[:, 0, block * TILE : (block + 1) * TILE]
        base[block] = smooth * (near * here - around)

    swap.wait_send()
    total = terms[me]
    for step in range(parts - 1):
        scatters[step].wait_recv()
        total = total + arrived[step]
    for k in range(k_count):
        product_rows = pl.ds(k * blocks_here, blocks_here)
        partial[product_rows, :] = total[:, k * TILE : (k + 1) * TILE]
    for block in range(blocks_here):
        summed = partial[pl.ds(block, k_count, stride=blocks_here), :]
        gradient_out[:, 0, block * TILE : (block + 1) * TILE] = summed + base[block]

    for copy in gathers + scatters:
        copy.wait_send()
    share.wait_send()


def local(
    fluence,
    tile_values,
    tile_rows,
    tile_columns,
    tile_count,
    labels,
    prescribed,
    weights,
    smoothing,
    beam_neighbours,
):
    groups = lax.axis_size("beam")
    parts = lax.axis_size("vox")
    k_count, _, shard = fluence.shape
    blocks_here = shard // TILE
    column_blocks = blocks_here * parts
    row_blocks = labels.shape[0] // TILE
    slots = tile_values.shape[2]
    chunks = 4
    vmem = pl.BlockSpec(memory_space=pltpu.VMEM)
    smem = pl.BlockSpec(memory_space=pltpu.SMEM)
    dma = pltpu.SemaphoreType.DMA
    return pl.pallas_call(
        functools.partial(kernel, parts, groups),
        out_shape=(
            jax.ShapeDtypeStruct((k_count, row_blocks * TILE), F32),
            jax.ShapeDtypeStruct(fluence.shape, F32),
        ),
        in_specs=[
            vmem,
            pl.BlockSpec(memory_space=pl.ANY),
            smem,
            smem,
            vmem,
            vmem,
            smem,
            vmem,
            smem,
            smem,
            smem,
            smem,
        ],
        out_specs=(vmem, vmem),
        scratch_shapes=[
            pltpu.VMEM((slots, TILE, TILE), F32),
            pltpu.VMEM((slots, 2 * TILE, TILE), BF16),
            pltpu.VMEM((column_blocks, k_count, TILE), F32),
            pltpu.VMEM((column_blocks, k_count, TILE), F32),
            pltpu.VMEM((k_count * slots, TILE), F32),
            pltpu.VMEM((k_count * row_blocks, TILE), F32),
            pltpu.VMEM((k_count * row_blocks, TILE), F32),
            pltpu.VMEM((row_blocks, k_count, TILE), F32),
            pltpu.VMEM((parts, blocks_here, k_count * TILE), F32),
            pltpu.VMEM((parts - 1, blocks_here, k_count * TILE), F32),
            pltpu.VMEM((blocks_here, k_count, TILE), F32),
            dma((chunks,)),
            dma((parts - 1,)),
            dma((parts - 1,)),
            dma((2,)),
            dma((2,)),
            dma((parts - 1,)),
            dma((parts - 1,)),
        ],
        compiler_params=pltpu.CompilerParams(
            collective_id=0, has_side_effects=True, vmem_limit_bytes=40 * 1024 * 1024
        ),
    )(
        fluence,
        tile_values,
        tile_rows,
        tile_columns,
        tile_rows,
        tile_columns,
        tile_count,
        labels.reshape(row_blocks, TILE),
        prescribed,
        weights,
        smoothing,
        beam_neighbours,
    )


def solution(mesh):
    return jax.shard_map(
        local,
        mesh=mesh,
        in_specs=(
            P("plans", "beam", "vox"),
            P(("plans", "vox"), "beam", None, None, None),
            P(("plans", "vox"), "beam", None),
            P(("plans", "vox"), "beam", None),
            P(("plans", "vox"), "beam"),
            P(("plans", "vox")),
            P("plans"),
            P("plans", None),
            P("plans"),
            P("plans", None),
        ),
        out_specs=(P("plans", "vox"), P("plans", "beam", "vox")),
        check_vma=False,
    )
```

```python
import functools

import jax
import jax.numpy as jnp
from jax import lax
from jax.experimental import pallas as pl
from jax.experimental.pallas import tpu as pltpu
from jax.sharding import PartitionSpec as P

TILE = 128
BLB = 512
MESH = pl.DeviceIdType.MESH
F32 = jnp.float32
BF16 = jnp.bfloat16


def two_terms(x):
    high = x.astype(BF16)
    return high, (x - high.astype(F32)).astype(BF16)


def three_terms(x):
    high = x.astype(BF16)
    rest = x - high.astype(F32)
    middle = rest.astype(BF16)
    return high, middle, (rest - middle.astype(F32)).astype(BF16)


def dot(a, b, on=0):
    return lax.dot_general(a, b, (((1,), (on,)), ((), ())), preferred_element_type=F32)


def kernel(
    wide_parts,
    tall_parts,
    groups,
    fluence_in,
    values,
    row_in,
    column_in,
    count_in,
    labels_in,
    prescribed_in,
    weights_in,
    smoothing_in,
    neighbours_in,
    dose_out,
    gradient_out,
    fluence,
    row_list,
    column_list,
    row_vector,
    column_vector,
    count,
    labels,
    prescribed,
    weights,
    smoothing,
    neighbours,
    tiles,
    split,
    own,
    other,
    product,
    partial,
    partner_partial,
    target,
    scaled,
    residual,
    terms,
    beside_terms,
    middle_terms,
    far_terms,
    base,
    small_sem,
    load_sem,
    tall_send,
    tall_recv,
    wide_send,
    wide_recv,
    pair_send,
    pair_recv,
    first_send,
    first_recv,
    second_send,
    second_recv,
):
    me = lax.axis_index("vox")
    group = lax.axis_index("beam")
    partner = lax.rem(group + 1, groups)
    tall, wide = me // wide_parts, me % wide_parts
    k_count = fluence.shape[0]
    blocks_here = fluence.shape[2] // TILE
    row_blocks = labels.shape[0]
    slots = tiles.shape[0]
    column_blocks = own.shape[0]
    structures = prescribed.shape[0]
    chunks = load_sem.shape[0]
    chunk = slots // chunks
    tall_at = [lax.rem(tall + step, tall_parts) for step in range(tall_parts)]
    tall_from = [lax.rem(tall + tall_parts - step, tall_parts) for step in range(tall_parts)]
    tall_peers = [at * wide_parts + wide for at in tall_at]
    wide_peers = [
        tall * wide_parts + lax.rem(wide + step, wide_parts) for step in range(wide_parts)
    ]

    def remote(source, target_ref, send, recv, axis, peer):
        copy = pltpu.make_async_remote_copy(
            src_ref=source,
            dst_ref=target_ref,
            send_sem=send,
            recv_sem=recv,
            device_id={axis: peer},
            device_id_type=MESH,
        )
        copy.start()
        return copy

    barrier = pltpu.get_barrier_semaphore()
    for peer in tall_peers[1:] + wide_peers[1:]:
        pl.semaphore_signal(barrier, inc=1, device_id={"vox": peer}, device_id_type=MESH)
    pl.semaphore_signal(barrier, inc=1, device_id={"beam": partner}, device_id_type=MESH)

    small = []
    for index, (source, place) in enumerate(
        (
            (fluence_in, fluence),
            (labels_in, labels),
            (prescribed_in, prescribed),
            (weights_in, weights),
            (column_in, column_list),
            (column_in, column_vector),
            (row_in, row_list),
            (row_in, row_vector),
            (count_in, count),
            (smoothing_in, smoothing),
            (neighbours_in, neighbours),
        )
    ):
        copy = pltpu.make_async_copy(source, place, small_sem.at[index])
        copy.start()
        small.append(copy)
    loads = []
    for part in range(chunks):
        here = pl.ds(part * chunk, chunk)
        copy = pltpu.make_async_copy(values.at[0, 0, here], tiles.at[here], load_sem.at[part])
        copy.start()
        loads.append(copy)

    small[0].wait()
    for block in range(blocks_here):
        own[me * blocks_here + block] = fluence[:, 0, block * TILE : (block + 1) * TILE]

    pl.semaphore_wait(barrier, tall_parts + wide_parts - 1)

    def shard_of(part):
        return own.at[pl.ds(part * blocks_here, blocks_here)]

    def along_wide(step, part):
        return [
            remote(
                shard_of(part),
                shard_of(part),
                wide_send.at[step, near],
                wide_recv.at[step, near],
                "vox",
                wide_peers[near + 1],
            )
            for near in range(wide_parts - 1)
        ]

    tall_copies = [
        remote(
            shard_of(me),
            shard_of(me),
            tall_send.at[step - 1],
            tall_recv.at[step - 1],
            "vox",
            tall_peers[step],
        )
        for step in range(1, tall_parts)
    ]
    wide_copies = along_wide(0, me)

    def split_chunk(part):
        loads[part].wait()
        for slot in range(part * chunk, (part + 1) * chunk):
            high, low = two_terms(tiles[slot])
            split[slot, :TILE] = high
            split[slot, TILE:] = low

    for copy in small[1:]:
        copy.wait()
    k_index = lax.broadcasted_iota(jnp.int32, (k_count, TILE), 0)

    def spread_over_k(read):
        column = jnp.zeros((k_count, TILE), F32)
        for k in range(k_count):
            column = jnp.where(k_index == k, read(k), column)
        return column

    def structure_values():
        weight_of = [spread_over_k(lambda k, s=s: weights[s, k]) for s in range(structures)]
        for row in range(row_blocks):
            label = jnp.broadcast_to(labels[row : row + 1, :], (k_count, TILE))
            level = jnp.zeros((k_count, TILE), F32)
            factor = jnp.zeros((k_count, TILE), F32)
            for structure in range(structures):
                member = label == structure
                level = jnp.where(member, prescribed[structure], level)
                factor = jnp.where(member, weight_of[structure], factor)
            target[row] = level
            scaled[row] = factor

    for part in range(chunks // 2):
        split_chunk(part)
    work = [functools.partial(split_chunk, part) for part in range(chunks // 2, chunks)]
    work.append(structure_values)
    for step in range(1, tall_parts):
        tall_copies[step - 1].wait_recv()
        wide_copies += along_wide(step, tall_from[step] * wide_parts + wide)
        if work:
            work.pop(0)()
    for piece in work:
        piece()
    for copy in wide_copies:
        copy.wait_recv()

    share = remote(own, other, pair_send.at[0], pair_recv.at[0], "beam", partner)

    for slot in range(slots):
        high, low = two_terms(own[column_list[0, 0, slot]])
        out = dot(jnp.concatenate([high, low], axis=0), split[slot], on=1)
        out = out[:k_count] + out[k_count:]
        product[pl.ds(slot, k_count, stride=slots), :] = out[:, :TILE] + out[:, TILE:]

    active = lax.broadcasted_iota(jnp.int32, (1, slots), 1) < count[0, 0]

    def products():
        return three_terms(
            jnp.concatenate(
                [product[k * slots : (k + 1) * slots, :] for k in range(k_count)], axis=1
            )
        )

    def placed(vector, blocks, three):
        place = jnp.where((vector == blocks) & active, 1.0, 0.0).astype(BF16)
        high, middle, low = three
        return dot(place, high) + (dot(place, middle) + dot(place, low))

    dose = placed(
        row_vector[0], lax.broadcasted_iota(jnp.int32, (row_blocks, slots), 0), products()
    )
    for k in range(k_count):
        partial[k * row_blocks : (k + 1) * row_blocks, :] = dose[:, k * TILE : (k + 1) * TILE]
    swap = remote(partial, partner_partial, pair_send.at[1], pair_recv.at[1], "beam", partner)
    swap.wait_recv()
    for row in range(row_blocks):
        where = pl.ds(row, k_count, stride=row_blocks)
        total = partial[where, :] + partner_partial[where, :]
        dose_out[:, row * TILE : (row + 1) * TILE] = total
        label = jnp.broadcast_to(labels[row : row + 1, :], (k_count, TILE))
        excess = total - target[row]
        excess = jnp.where(label == 0, excess, jnp.maximum(excess, 0.0))
        residual[row] = scaled[row] * excess

    for slot in range(slots):
        high, low = two_terms(residual[row_list[0, 0, slot]])
        both = jnp.concatenate([high, low], axis=0)
        out = dot(jnp.concatenate([both, both], axis=1), split[slot])
        product[pl.ds(slot, k_count, stride=slots), :] = out[:k_count] + out[k_count:]

    three = products()
    line = lax.broadcasted_iota(jnp.int32, (tall_parts * blocks_here, slots), 0)
    line_tall, line_block = line // blocks_here, line % blocks_here

    def make_terms(near):
        at = lax.rem(wide + near, wide_parts)
        found = placed(column_vector[0], (line_tall * wide_parts + at) * blocks_here + line_block, three)
        for part in range(tall_parts):
            terms[near, part] = found[part * blocks_here : (part + 1) * blocks_here, :]

    steps = list(range(1, tall_parts)) + [0]
    first_copies = {step: [] for step in steps}
    for near in range(1, wide_parts):
        make_terms(near)
        for step in steps:
            first_copies[step].append(
                remote(
                    terms.at[near, tall_at[step]],
                    beside_terms.at[step, near - 1],
                    first_send.at[step, near - 1],
                    first_recv.at[step, near - 1],
                    "vox",
                    wide_peers[near],
                )
            )
    make_terms(0)

    def gathered(step):
        total = terms[0, tall_at[step]]
        for near, copy in enumerate(first_copies[step]):
            copy.wait_recv()
            total = total + beside_terms[step, near]
        return total

    second_copies = []
    for step in range(1, tall_parts):
        middle_terms[step - 1] = gathered(step)
        second_copies.append(
            remote(
                middle_terms.at[step - 1],
                far_terms.at[step - 1],
                second_send.at[step - 1],
                second_recv.at[step - 1],
                "vox",
                tall_peers[step],
            )
        )

    share.wait_recv()
    smooth = spread_over_k(lambda k: smoothing[k])
    per_beam = BLB // TILE
    group_beams = column_blocks // per_beam
    near_count = neighbours.shape[0]
    for block in range(blocks_here):
        place = group * column_blocks + me * blocks_here + block
        beam = place // per_beam
        within = place % per_beam
        around = jnp.zeros((k_count, TILE), F32)
        for n in range(near_count):
            beside = neighbours[n, beam]
            beside_group = jnp.where(beside >= group_beams, 1, 0)
            at = (beside - beside_group * group_beams) * per_beam + within
            around = around + jnp.where(beside_group == group, own[at], other[at])
        here = fluence[:, 0, block * TILE : (block + 1) * TILE]
        base[block] = smooth * (near_count * here - around)

    swap.wait_send()
    total = gathered(0)
    for copy_index, copy in enumerate(second_copies):
        copy.wait_recv()
        total = total + far_terms[copy_index]
    for k in range(k_count):
        partial[k * blocks_here : (k + 1) * blocks_here, :] = total[:, k * TILE : (k + 1) * TILE]
    for block in range(blocks_here):
        summed = partial[pl.ds(block, k_count, stride=blocks_here), :]
        gradient_out[:, 0, block * TILE : (block + 1) * TILE] = summed + base[block]

    for copy in tall_copies + wide_copies + second_copies + [share]:
        copy.wait_send()
    for copies in first_copies.values():
        for copy in copies:
            copy.wait_send()


def local(
    fluence,
    tile_values,
    tile_rows,
    tile_columns,
    tile_count,
    labels,
    prescribed,
    weights,
    smoothing,
    beam_neighbours,
):
    groups = lax.axis_size("beam")
    parts = lax.axis_size("vox")
    wide_parts = max(w for w in range(1, parts + 1) if parts % w == 0 and w * w <= parts)
    tall_parts = parts // wide_parts
    k_count, _, shard = fluence.shape
    blocks_here = shard // TILE
    column_blocks = blocks_here * parts
    row_blocks = labels.shape[0] // TILE
    slots = tile_values.shape[2]
    chunks = 4
    width = k_count * TILE
    operands = (
        fluence,
        tile_values,
        tile_rows,
        tile_columns,
        tile_count,
        labels.reshape(row_blocks, TILE),
        prescribed,
        weights.T,
        smoothing,
        beam_neighbours.T,
    )

    def on_chip(array, space):
        return space(array.shape, array.dtype)

    vmem, smem = pltpu.VMEM, pltpu.SMEM
    dma = pltpu.SemaphoreType.DMA
    out = pl.BlockSpec(memory_space=pltpu.VMEM)
    return pl.pallas_call(
        functools.partial(kernel, wide_parts, tall_parts, groups),
        out_shape=(
            jax.ShapeDtypeStruct((k_count, row_blocks * TILE), F32),
            jax.ShapeDtypeStruct(fluence.shape, F32),
        ),
        in_specs=[pl.BlockSpec(memory_space=pltpu.HBM)] * len(operands),
        out_specs=(out, out),
        scratch_shapes=[
            on_chip(fluence, vmem),
            on_chip(tile_rows, smem),
            on_chip(tile_columns, smem),
            on_chip(tile_rows, vmem),
            on_chip(tile_columns, vmem),
            on_chip(tile_count, smem),
            on_chip(operands[5], vmem),
            on_chip(prescribed, smem),
            on_chip(operands[7], smem),
            on_chip(smoothing, smem),
            on_chip(operands[9], smem),
            vmem((slots, TILE, TILE), F32),
            vmem((slots, 2 * TILE, TILE), BF16),
            vmem((column_blocks, k_count, TILE), F32),
            vmem((column_blocks, k_count, TILE), F32),
            vmem((k_count * slots, TILE), F32),
            vmem((k_count * row_blocks, TILE), F32),
            vmem((k_count * row_blocks, TILE), F32),
            vmem((row_blocks, k_count, TILE), F32),
            vmem((row_blocks, k_count, TILE), F32),
            vmem((row_blocks, k_count, TILE), F32),
            vmem((wide_parts, tall_parts, blocks_here, width), F32),
            vmem((tall_parts, wide_parts - 1, blocks_here, width), F32),
            vmem((tall_parts - 1, blocks_here, width), F32),
            vmem((tall_parts - 1, blocks_here, width), F32),
            vmem((blocks_here, k_count, TILE), F32),
            dma((11,)),
            dma((chunks,)),
            dma((tall_parts - 1,)),
            dma((tall_parts - 1,)),
            dma((tall_parts, wide_parts - 1)),
            dma((tall_parts, wide_parts - 1)),
            dma((2,)),
            dma((2,)),
            dma((tall_parts, wide_parts - 1)),
            dma((tall_parts, wide_parts - 1)),
            dma((tall_parts - 1,)),
            dma((tall_parts - 1,)),
        ],
        compiler_params=pltpu.CompilerParams(
            collective_id=0, has_side_effects=True, vmem_limit_bytes=58 * 1024 * 1024
        ),
    )(*operands)


def solution(mesh):
    return jax.shard_map(
        local,
        mesh=mesh,
        in_specs=(
            P("plans", "beam", "vox"),
            P(("plans", "vox"), "beam", None, None, None),
            P(("plans", "vox"), "beam", None),
            P(("plans", "vox"), "beam", None),
            P(("plans", "vox"), "beam"),
            P(("plans", "vox")),
            P("plans"),
            P("plans", None),
            P("plans"),
            P("plans", None),
        ),
        out_specs=(P("plans", "vox"), P("plans", "beam", "vox")),
        check_vma=False,
    )
```

```python
import functools

import jax
import jax.numpy as jnp
from jax import lax
from jax.experimental import pallas as pl
from jax.experimental.pallas import tpu as pltpu
from jax.sharding import PartitionSpec as P

TILE = 128
BLB = 512
MESH = pl.DeviceIdType.MESH
F32 = jnp.float32
BF16 = jnp.bfloat16


def two_terms(x):
    high = x.astype(BF16)
    return high, (x - high.astype(F32)).astype(BF16)


def three_terms(x):
    high = x.astype(BF16)
    rest = x - high.astype(F32)
    middle = rest.astype(BF16)
    return high, middle, (rest - middle.astype(F32)).astype(BF16)


def dot(a, b, on=0):
    return lax.dot_general(a, b, (((1,), (on,)), ((), ())), preferred_element_type=F32)


def kernel(
    wide_parts,
    tall_parts,
    groups,
    fluence_in,
    values,
    row_in,
    column_in,
    count_in,
    labels_in,
    prescribed_in,
    weights_in,
    smoothing_in,
    neighbours_in,
    dose_out,
    gradient_out,
    fluence,
    row_list,
    column_list,
    row_vector,
    column_vector,
    count,
    labels,
    prescribed,
    weights,
    smoothing,
    neighbours,
    tiles,
    split,
    own,
    other,
    product,
    partial,
    partner_partial,
    target,
    scaled,
    residual,
    terms,
    beside_terms,
    middle_terms,
    far_terms,
    base,
    small_sem,
    load_sem,
    tall_send,
    tall_recv,
    wide_send,
    wide_recv,
    pair_send,
    pair_recv,
    first_send,
    first_recv,
    second_send,
    second_recv,
):
    me = lax.axis_index("vox")
    group = lax.axis_index("beam")
    partner = lax.rem(group + 1, groups)
    tall, wide = me // wide_parts, me % wide_parts
    k_count = fluence.shape[0]
    blocks_here = fluence.shape[2] // TILE
    row_blocks = labels.shape[0]
    slots = tiles.shape[0]
    column_blocks = own.shape[0]
    structures = prescribed.shape[0]
    chunks = load_sem.shape[0]
    chunk = slots // chunks
    tall_at = [lax.rem(tall + step, tall_parts) for step in range(tall_parts)]
    tall_from = [lax.rem(tall + tall_parts - step, tall_parts) for step in range(tall_parts)]
    tall_peers = [at * wide_parts + wide for at in tall_at]
    wide_peers = [
        tall * wide_parts + lax.rem(wide + step, wide_parts) for step in range(wide_parts)
    ]

    def remote(source, target_ref, send, recv, axis, peer):
        copy = pltpu.make_async_remote_copy(
            src_ref=source,
            dst_ref=target_ref,
            send_sem=send,
            recv_sem=recv,
            device_id={axis: peer},
            device_id_type=MESH,
        )
        copy.start()
        return copy

    barrier = pltpu.get_barrier_semaphore()
    for peer in tall_peers[1:] + wide_peers[1:]:
        pl.semaphore_signal(barrier, inc=1, device_id={"vox": peer}, device_id_type=MESH)
    pl.semaphore_signal(barrier, inc=1, device_id={"beam": partner}, device_id_type=MESH)

    small = []
    for index, (source, place) in enumerate(
        (
            (fluence_in, fluence),
            (labels_in, labels),
            (prescribed_in, prescribed),
            (weights_in, weights),
            (column_in, column_list),
            (column_in, column_vector),
            (row_in, row_list),
            (row_in, row_vector),
            (count_in, count),
            (smoothing_in, smoothing),
            (neighbours_in, neighbours),
        )
    ):
        copy = pltpu.make_async_copy(source, place, small_sem.at[index])
        copy.start()
        small.append(copy)
    loads = []
    for part in range(chunks):
        here = pl.ds(part * chunk, chunk)
        copy = pltpu.make_async_copy(values.at[0, 0, here], tiles.at[here], load_sem.at[part])
        copy.start()
        loads.append(copy)

    small[0].wait()
    for block in range(blocks_here):
        own[me * blocks_here + block] = fluence[:, 0, block * TILE : (block + 1) * TILE]

    pl.semaphore_wait(barrier, tall_parts + wide_parts - 1)

    def shard_of(part):
        return own.at[pl.ds(part * blocks_here, blocks_here)]

    def along_wide(step, part):
        return [
            remote(
                shard_of(part),
                shard_of(part),
                wide_send.at[step, near],
                wide_recv.at[step, near],
                "vox",
                wide_peers[near + 1],
            )
            for near in range(wide_parts - 1)
        ]

    tall_copies = [
        remote(
            shard_of(me),
            shard_of(me),
            tall_send.at[step - 1],
            tall_recv.at[step - 1],
            "vox",
            tall_peers[step],
        )
        for step in range(1, tall_parts)
    ]
    wide_copies = along_wide(0, me)

    def split_chunk(part):
        loads[part].wait()
        for slot in range(part * chunk, (part + 1) * chunk):
            high, low = two_terms(tiles[slot])
            split[slot, :TILE] = high
            split[slot, TILE:] = low

    for copy in small[1:]:
        copy.wait()
    k_index = lax.broadcasted_iota(jnp.int32, (k_count, TILE), 0)

    def spread_over_k(read):
        column = jnp.zeros((k_count, TILE), F32)
        for k in range(k_count):
            column = jnp.where(k_index == k, read(k), column)
        return column

    def structure_values():
        weight_of = [spread_over_k(lambda k, s=s: weights[s, k]) for s in range(structures)]
        for row in range(row_blocks):
            label = jnp.broadcast_to(labels[row : row + 1, :], (k_count, TILE))
            level = jnp.zeros((k_count, TILE), F32)
            factor = jnp.zeros((k_count, TILE), F32)
            for structure in range(structures):
                member = label == structure
                level = jnp.where(member, prescribed[structure], level)
                factor = jnp.where(member, weight_of[structure], factor)
            target[row] = level
            scaled[row] = factor

    for part in range(chunks // 2):
        split_chunk(part)
    work = [functools.partial(split_chunk, part) for part in range(chunks // 2, chunks)]
    work.append(structure_values)
    for step in range(1, tall_parts):
        tall_copies[step - 1].wait_recv()
        wide_copies += along_wide(step, tall_from[step] * wide_parts + wide)
        if work:
            work.pop(0)()
    for piece in work:
        piece()
    for copy in wide_copies:
        copy.wait_recv()

    share = remote(own, other, pair_send.at[0], pair_recv.at[0], "beam", partner)

    for slot in range(slots):
        high, low = two_terms(own[column_list[0, 0, slot]])
        out = dot(jnp.concatenate([high, low], axis=0), split[slot], on=1)
        out = out[:k_count] + out[k_count:]
        product[pl.ds(slot, k_count, stride=slots), :] = out[:, :TILE] + out[:, TILE:]

    active = lax.broadcasted_iota(jnp.int32, (1, slots), 1) < count[0, 0]

    def products():
        return three_terms(
            jnp.concatenate(
                [product[k * slots : (k + 1) * slots, :] for k in range(k_count)], axis=1
            )
        )

    def placed(vector, blocks, three):
        place = jnp.where((vector == blocks) & active, 1.0, 0.0).astype(BF16)
        high, middle, low = three
        return dot(place, high) + (dot(place, middle) + dot(place, low))

    dose = placed(
        row_vector[0], lax.broadcasted_iota(jnp.int32, (row_blocks, slots), 0), products()
    )
    for k in range(k_count):
        partial[k * row_blocks : (k + 1) * row_blocks, :] = dose[:, k * TILE : (k + 1) * TILE]
    swap = remote(partial, partner_partial, pair_send.at[1], pair_recv.at[1], "beam", partner)
    swap.wait_recv()
    for row in range(row_blocks):
        where = pl.ds(row, k_count, stride=row_blocks)
        total = partial[where, :] + partner_partial[where, :]
        dose_out[:, row * TILE : (row + 1) * TILE] = total
        label = jnp.broadcast_to(labels[row : row + 1, :], (k_count, TILE))
        excess = total - target[row]
        excess = jnp.where(label == 0, excess, jnp.maximum(excess, 0.0))
        residual[row] = scaled[row] * excess

    for slot in range(slots):
        high, low = two_terms(residual[row_list[0, 0, slot]])
        both = jnp.concatenate([high, low], axis=0)
        out = dot(jnp.concatenate([both, both], axis=1), split[slot])
        product[pl.ds(slot, k_count, stride=slots), :] = out[:k_count] + out[k_count:]

    three = products()
    line = lax.broadcasted_iota(jnp.int32, (tall_parts * blocks_here, slots), 0)
    line_tall, line_block = line // blocks_here, line % blocks_here

    def make_terms(near):
        at = lax.rem(wide + near, wide_parts)
        found = placed(column_vector[0], (line_tall * wide_parts + at) * blocks_here + line_block, three)
        for part in range(tall_parts):
            terms[near, part] = found[part * blocks_here : (part + 1) * blocks_here, :]

    steps = list(range(1, tall_parts)) + [0]
    first_copies = {step: [] for step in steps}
    for near in range(1, wide_parts):
        make_terms(near)
        for step in steps:
            first_copies[step].append(
                remote(
                    terms.at[near, tall_at[step]],
                    beside_terms.at[step, near - 1],
                    first_send.at[step, near - 1],
                    first_recv.at[step, near - 1],
                    "vox",
                    wide_peers[near],
                )
            )
    make_terms(0)

    def gathered(step):
        total = terms[0, tall_at[step]]
        for near, copy in enumerate(first_copies[step]):
            copy.wait_recv()
            total = total + beside_terms[step, near]
        return total

    second_copies = []
    for step in range(1, tall_parts):
        middle_terms[step - 1] = gathered(step)
        second_copies.append(
            remote(
                middle_terms.at[step - 1],
                far_terms.at[step - 1],
                second_send.at[step - 1],
                second_recv.at[step - 1],
                "vox",
                tall_peers[step],
            )
        )

    share.wait_recv()
    smooth = spread_over_k(lambda k: smoothing[k])
    per_beam = BLB // TILE
    group_beams = column_blocks // per_beam
    near_count = neighbours.shape[0]
    for block in range(blocks_here):
        place = group * column_blocks + me * blocks_here + block
        beam = place // per_beam
        within = place % per_beam
        around = jnp.zeros((k_count, TILE), F32)
        for n in range(near_count):
            beside = neighbours[n, beam]
            beside_group = jnp.where(beside >= group_beams, 1, 0)
            at = (beside - beside_group * group_beams) * per_beam + within
            around = around + jnp.where(beside_group == group, own[at], other[at])
        here = fluence[:, 0, block * TILE : (block + 1) * TILE]
        base[block] = smooth * (near_count * here - around)

    swap.wait_send()
    total = gathered(0)
    for copy_index, copy in enumerate(second_copies):
        copy.wait_recv()
        total = total + far_terms[copy_index]
    for k in range(k_count):
        partial[k * blocks_here : (k + 1) * blocks_here, :] = total[:, k * TILE : (k + 1) * TILE]
    for block in range(blocks_here):
        summed = partial[pl.ds(block, k_count, stride=blocks_here), :]
        gradient_out[:, 0, block * TILE : (block + 1) * TILE] = summed + base[block]

    for copy in tall_copies + wide_copies + second_copies + [share]:
        copy.wait_send()
    for copies in first_copies.values():
        for copy in copies:
            copy.wait_send()


def local(
    fluence,
    tile_values,
    tile_rows,
    tile_columns,
    tile_count,
    labels,
    prescribed,
    weights,
    smoothing,
    beam_neighbours,
):
    groups = lax.axis_size("beam")
    parts = lax.axis_size("vox")
    wide_parts = max(w for w in range(1, parts + 1) if parts % w == 0 and w * w <= parts)
    tall_parts = parts // wide_parts
    k_count, _, shard = fluence.shape
    blocks_here = shard // TILE
    column_blocks = blocks_here * parts
    row_blocks = labels.shape[0] // TILE
    slots = tile_values.shape[2]
    chunks = 4
    width = k_count * TILE
    operands = (
        fluence,
        tile_values,
        tile_rows,
        tile_columns,
        tile_count,
        labels.reshape(row_blocks, TILE),
        prescribed,
        weights.T,
        smoothing,
        beam_neighbours.T,
    )

    def on_chip(array, space):
        return space(array.shape, array.dtype)

    vmem, smem = pltpu.VMEM, pltpu.SMEM
    dma = pltpu.SemaphoreType.DMA
    out = pl.BlockSpec(memory_space=pltpu.VMEM)
    return pl.pallas_call(
        functools.partial(kernel, wide_parts, tall_parts, groups),
        out_shape=(
            jax.ShapeDtypeStruct((k_count, row_blocks * TILE), F32),
            jax.ShapeDtypeStruct(fluence.shape, F32),
        ),
        in_specs=[pl.BlockSpec(memory_space=pltpu.HBM)] * len(operands),
        out_specs=(out, out),
        scratch_shapes=[
            on_chip(fluence, vmem),
            on_chip(tile_rows, smem),
            on_chip(tile_columns, smem),
            on_chip(tile_rows, vmem),
            on_chip(tile_columns, vmem),
            on_chip(tile_count, smem),
            on_chip(operands[5], vmem),
            on_chip(prescribed, smem),
            on_chip(operands[7], smem),
            on_chip(smoothing, smem),
            on_chip(operands[9], smem),
            vmem((slots, TILE, TILE), F32),
            vmem((slots, 2 * TILE, TILE), BF16),
            vmem((column_blocks, k_count, TILE), F32),
            vmem((column_blocks, k_count, TILE), F32),
            vmem((k_count * slots, TILE), F32),
            vmem((k_count * row_blocks, TILE), F32),
            vmem((k_count * row_blocks, TILE), F32),
            vmem((row_blocks, k_count, TILE), F32),
            vmem((row_blocks, k_count, TILE), F32),
            vmem((row_blocks, k_count, TILE), F32),
            vmem((wide_parts, tall_parts, blocks_here, width), F32),
            vmem((tall_parts, wide_parts - 1, blocks_here, width), F32),
            vmem((tall_parts - 1, blocks_here, width), F32),
            vmem((tall_parts - 1, blocks_here, width), F32),
            vmem((blocks_here, k_count, TILE), F32),
            dma((11,)),
            dma((chunks,)),
            dma((tall_parts - 1,)),
            dma((tall_parts - 1,)),
            dma((tall_parts, wide_parts - 1)),
            dma((tall_parts, wide_parts - 1)),
            dma((2,)),
            dma((2,)),
            dma((tall_parts, wide_parts - 1)),
            dma((tall_parts, wide_parts - 1)),
            dma((tall_parts - 1,)),
            dma((tall_parts - 1,)),
        ],
        compiler_params=pltpu.CompilerParams(
            collective_id=0, has_side_effects=True, vmem_limit_bytes=40 * 1024 * 1024
        ),
    )(*[x if x is tile_count else pltpu.with_memory_space_constraint(x, pltpu.HBM) for x in operands])


def solution(mesh):
    return jax.shard_map(
        local,
        mesh=mesh,
        in_specs=(
            P("plans", "beam", "vox"),
            P(("plans", "vox"), "beam", None, None, None),
            P(("plans", "vox"), "beam", None),
            P(("plans", "vox"), "beam", None),
            P(("plans", "vox"), "beam"),
            P(("plans", "vox")),
            P("plans"),
            P("plans", None),
            P("plans"),
            P("plans", None),
        ),
        out_specs=(P("plans", "vox"), P("plans", "beam", "vox")),
        check_vma=False,
    )
```

```python
import functools

import jax
import jax.numpy as jnp
from jax import lax
from jax.experimental import pallas as pl
from jax.experimental.pallas import tpu as pltpu
from jax.sharding import PartitionSpec as P

TILE = 128
BLB = 512
MESH = pl.DeviceIdType.MESH
F32 = jnp.float32
BF16 = jnp.bfloat16


def two_terms(x):
    high = x.astype(BF16)
    return high, (x - high.astype(F32)).astype(BF16)


def three_terms(x):
    high = x.astype(BF16)
    rest = x - high.astype(F32)
    middle = rest.astype(BF16)
    return high, middle, (rest - middle.astype(F32)).astype(BF16)


def dot(a, b, on=0):
    return lax.dot_general(a, b, (((1,), (on,)), ((), ())), preferred_element_type=F32)


def kernel(
    wide_parts,
    tall_parts,
    groups,
    fluence_in,
    values,
    row_in,
    column_in,
    count_in,
    labels_in,
    prescribed_in,
    weights_in,
    smoothing_in,
    neighbours_in,
    dose_out,
    gradient_out,
    fluence,
    row_list,
    column_list,
    row_vector,
    column_vector,
    count,
    labels,
    prescribed,
    weights,
    smoothing,
    neighbours,
    tiles,
    split,
    own,
    other,
    product,
    partial,
    partner_partial,
    target,
    scaled,
    residual,
    terms,
    beside_terms,
    middle_terms,
    far_terms,
    base,
    small_sem,
    load_sem,
    tall_send,
    tall_recv,
    wide_send,
    wide_recv,
    pair_send,
    pair_recv,
    first_send,
    first_recv,
    second_send,
    second_recv,
):
    me = lax.axis_index("vox")
    group = lax.axis_index("beam")
    partner = lax.rem(group + 1, groups)
    tall, wide = me // wide_parts, me % wide_parts
    k_count = fluence.shape[0]
    blocks_here = fluence.shape[2] // TILE
    row_blocks = labels.shape[0]
    slots = tiles.shape[0]
    column_blocks = own.shape[0]
    structures = prescribed.shape[0]
    chunks = load_sem.shape[0]
    chunk = slots // chunks
    tall_at = [lax.rem(tall + step, tall_parts) for step in range(tall_parts)]
    tall_from = [lax.rem(tall + tall_parts - step, tall_parts) for step in range(tall_parts)]
    tall_peers = [at * wide_parts + wide for at in tall_at]
    wide_peers = [
        tall * wide_parts + lax.rem(wide + step, wide_parts) for step in range(wide_parts)
    ]

    def remote(source, target_ref, send, recv, axis, peer):
        copy = pltpu.make_async_remote_copy(
            src_ref=source,
            dst_ref=target_ref,
            send_sem=send,
            recv_sem=recv,
            device_id={axis: peer},
            device_id_type=MESH,
        )
        copy.start()
        return copy

    barrier = pltpu.get_barrier_semaphore()
    for peer in tall_peers[1:] + wide_peers[1:]:
        pl.semaphore_signal(barrier, inc=1, device_id={"vox": peer}, device_id_type=MESH)
    pl.semaphore_signal(barrier, inc=1, device_id={"beam": partner}, device_id_type=MESH)

    small = []
    for index, (source, place) in enumerate(
        (
            (fluence_in, fluence),
            (labels_in, labels),
            (prescribed_in, prescribed),
            (weights_in, weights),
            (column_in, column_list),
            (column_in, column_vector),
            (row_in, row_list),
            (row_in, row_vector),
            (count_in, count),
            (smoothing_in, smoothing),
            (neighbours_in, neighbours),
        )
    ):
        copy = pltpu.make_async_copy(source, place, small_sem.at[index])
        copy.start()
        small.append(copy)
    loads = []
    for part in range(chunks):
        here = pl.ds(part * chunk, chunk)
        copy = pltpu.make_async_copy(values.at[0, 0, here], tiles.at[here], load_sem.at[part])
        copy.start()
        loads.append(copy)

    small[0].wait()
    for block in range(blocks_here):
        own[me * blocks_here + block] = fluence[:, 0, block * TILE : (block + 1) * TILE]

    pl.semaphore_wait(barrier, tall_parts + wide_parts - 1)

    pieces = tall_send.shape[1]
    piece_blocks = blocks_here // pieces

    def shard_of(part, piece):
        return own.at[pl.ds(part * blocks_here + piece * piece_blocks, piece_blocks)]

    def along_wide(step, part, piece):
        return [
            remote(
                shard_of(part, piece),
                shard_of(part, piece),
                wide_send.at[step, near, piece],
                wide_recv.at[step, near, piece],
                "vox",
                wide_peers[near + 1],
            )
            for near in range(wide_parts - 1)
        ]

    wide_copies = []
    tall_copies = {}
    for piece in range(pieces):
        wide_copies += along_wide(0, me, piece)
        for step in range(1, tall_parts):
            tall_copies[step, piece] = remote(
                shard_of(me, piece),
                shard_of(me, piece),
                tall_send.at[step - 1, piece],
                tall_recv.at[step - 1, piece],
                "vox",
                tall_peers[step],
            )

    def split_chunk(part):
        loads[part].wait()
        for slot in range(part * chunk, (part + 1) * chunk):
            high, low = two_terms(tiles[slot])
            split[slot, :TILE] = high
            split[slot, TILE:] = low

    for copy in small[1:]:
        copy.wait()
    k_index = lax.broadcasted_iota(jnp.int32, (k_count, TILE), 0)

    def spread_over_k(read):
        column = jnp.zeros((k_count, TILE), F32)
        for k in range(k_count):
            column = jnp.where(k_index == k, read(k), column)
        return column

    def structure_values():
        weight_of = [spread_over_k(lambda k, s=s: weights[s, k]) for s in range(structures)]
        for row in range(row_blocks):
            label = jnp.broadcast_to(labels[row : row + 1, :], (k_count, TILE))
            level = jnp.zeros((k_count, TILE), F32)
            factor = jnp.zeros((k_count, TILE), F32)
            for structure in range(structures):
                member = label == structure
                level = jnp.where(member, prescribed[structure], level)
                factor = jnp.where(member, weight_of[structure], factor)
            target[row] = level
            scaled[row] = factor

    for part in range(chunks // 2):
        split_chunk(part)
    work = [functools.partial(split_chunk, part) for part in range(chunks // 2, chunks)]
    work.append(structure_values)
    for piece in range(pieces):
        for step in range(1, tall_parts):
            tall_copies[step, piece].wait_recv()
            wide_copies += along_wide(step, tall_from[step] * wide_parts + wide, piece)
            if work:
                work.pop(0)()
    for piece in work:
        piece()
    for copy in wide_copies:
        copy.wait_recv()

    share = remote(own, other, pair_send.at[0], pair_recv.at[0], "beam", partner)

    for slot in range(slots):
        high, low = two_terms(own[column_list[0, 0, slot]])
        out = dot(jnp.concatenate([high, low], axis=0), split[slot], on=1)
        out = out[:k_count] + out[k_count:]
        product[pl.ds(slot, k_count, stride=slots), :] = out[:, :TILE] + out[:, TILE:]

    active = lax.broadcasted_iota(jnp.int32, (1, slots), 1) < count[0, 0]

    def products():
        return three_terms(
            jnp.concatenate(
                [product[k * slots : (k + 1) * slots, :] for k in range(k_count)], axis=1
            )
        )

    def placed(vector, blocks, three):
        place = jnp.where((vector == blocks) & active, 1.0, 0.0).astype(BF16)
        high, middle, low = three
        return dot(place, high) + (dot(place, middle) + dot(place, low))

    dose = placed(
        row_vector[0], lax.broadcasted_iota(jnp.int32, (row_blocks, slots), 0), products()
    )
    for k in range(k_count):
        partial[k * row_blocks : (k + 1) * row_blocks, :] = dose[:, k * TILE : (k + 1) * TILE]
    swap = remote(partial, partner_partial, pair_send.at[1], pair_recv.at[1], "beam", partner)
    swap.wait_recv()
    for row in range(row_blocks):
        where = pl.ds(row, k_count, stride=row_blocks)
        total = partial[where, :] + partner_partial[where, :]
        dose_out[:, row * TILE : (row + 1) * TILE] = total
        label = jnp.broadcast_to(labels[row : row + 1, :], (k_count, TILE))
        excess = total - target[row]
        excess = jnp.where(label == 0, excess, jnp.maximum(excess, 0.0))
        residual[row] = scaled[row] * excess

    for slot in range(slots):
        high, low = two_terms(residual[row_list[0, 0, slot]])
        both = jnp.concatenate([high, low], axis=0)
        out = dot(jnp.concatenate([both, both], axis=1), split[slot])
        product[pl.ds(slot, k_count, stride=slots), :] = out[:k_count] + out[k_count:]

    three = products()
    line = lax.broadcasted_iota(jnp.int32, (tall_parts * blocks_here, slots), 0)
    line_tall, line_block = line // blocks_here, line % blocks_here

    def make_terms(near):
        at = lax.rem(wide + near, wide_parts)
        found = placed(column_vector[0], (line_tall * wide_parts + at) * blocks_here + line_block, three)
        for part in range(tall_parts):
            terms[near, part] = found[part * blocks_here : (part + 1) * blocks_here, :]

    steps = list(range(1, tall_parts)) + [0]
    first_copies = {step: [] for step in steps}
    for near in range(1, wide_parts):
        make_terms(near)
        for step in steps:
            first_copies[step].append(
                remote(
                    terms.at[near, tall_at[step]],
                    beside_terms.at[step, near - 1],
                    first_send.at[step, near - 1],
                    first_recv.at[step, near - 1],
                    "vox",
                    wide_peers[near],
                )
            )
    make_terms(0)

    def gathered(step):
        total = terms[0, tall_at[step]]
        for near, copy in enumerate(first_copies[step]):
            copy.wait_recv()
            total = total + beside_terms[step, near]
        return total

    second_copies = []
    for step in range(1, tall_parts):
        middle_terms[step - 1] = gathered(step)
        second_copies.append(
            remote(
                middle_terms.at[step - 1],
                far_terms.at[step - 1],
                second_send.at[step - 1],
                second_recv.at[step - 1],
                "vox",
                tall_peers[step],
            )
        )

    share.wait_recv()
    smooth = spread_over_k(lambda k: smoothing[k])
    per_beam = BLB // TILE
    group_beams = column_blocks // per_beam
    near_count = neighbours.shape[0]
    for block in range(blocks_here):
        place = group * column_blocks + me * blocks_here + block
        beam = place // per_beam
        within = place % per_beam
        around = jnp.zeros((k_count, TILE), F32)
        for n in range(near_count):
            beside = neighbours[n, beam]
            beside_group = jnp.where(beside >= group_beams, 1, 0)
            at = (beside - beside_group * group_beams) * per_beam + within
            around = around + jnp.where(beside_group == group, own[at], other[at])
        here = fluence[:, 0, block * TILE : (block + 1) * TILE]
        base[block] = smooth * (near_count * here - around)

    swap.wait_send()
    total = gathered(0)
    for copy_index, copy in enumerate(second_copies):
        copy.wait_recv()
        total = total + far_terms[copy_index]
    for k in range(k_count):
        partial[k * blocks_here : (k + 1) * blocks_here, :] = total[:, k * TILE : (k + 1) * TILE]
    for block in range(blocks_here):
        summed = partial[pl.ds(block, k_count, stride=blocks_here), :]
        gradient_out[:, 0, block * TILE : (block + 1) * TILE] = summed + base[block]

    for copy in list(tall_copies.values()) + wide_copies + second_copies + [share]:
        copy.wait_send()
    for copies in first_copies.values():
        for copy in copies:
            copy.wait_send()


def local(
    fluence,
    tile_values,
    tile_rows,
    tile_columns,
    tile_count,
    labels,
    prescribed,
    weights,
    smoothing,
    beam_neighbours,
):
    groups = lax.axis_size("beam")
    parts = lax.axis_size("vox")
    wide_parts = max(w for w in range(1, parts + 1) if parts % w == 0 and w * w <= parts)
    tall_parts = parts // wide_parts
    k_count, _, shard = fluence.shape
    blocks_here = shard // TILE
    column_blocks = blocks_here * parts
    row_blocks = labels.shape[0] // TILE
    slots = tile_values.shape[2]
    chunks = 4
    pieces = 2 if blocks_here % 2 == 0 else 1
    width = k_count * TILE
    operands = (
        fluence,
        tile_values,
        tile_rows,
        tile_columns,
        tile_count,
        labels.reshape(row_blocks, TILE),
        prescribed,
        weights.T,
        smoothing,
        beam_neighbours.T,
    )

    def on_chip(array, space):
        return space(array.shape, array.dtype)

    vmem, smem = pltpu.VMEM, pltpu.SMEM
    dma = pltpu.SemaphoreType.DMA
    out = pl.BlockSpec(memory_space=pltpu.VMEM)
    return pl.pallas_call(
        functools.partial(kernel, wide_parts, tall_parts, groups),
        out_shape=(
            jax.ShapeDtypeStruct((k_count, row_blocks * TILE), F32),
            jax.ShapeDtypeStruct(fluence.shape, F32),
        ),
        in_specs=[pl.BlockSpec(memory_space=pltpu.HBM)] * len(operands),
        out_specs=(out, out),
        scratch_shapes=[
            on_chip(fluence, vmem),
            on_chip(tile_rows, smem),
            on_chip(tile_columns, smem),
            on_chip(tile_rows, vmem),
            on_chip(tile_columns, vmem),
            on_chip(tile_count, smem),
            on_chip(operands[5], vmem),
            on_chip(prescribed, smem),
            on_chip(operands[7], smem),
            on_chip(smoothing, smem),
            on_chip(operands[9], smem),
            vmem((slots, TILE, TILE), F32),
            vmem((slots, 2 * TILE, TILE), BF16),
            vmem((column_blocks, k_count, TILE), F32),
            vmem((column_blocks, k_count, TILE), F32),
            vmem((k_count * slots, TILE), F32),
            vmem((k_count * row_blocks, TILE), F32),
            vmem((k_count * row_blocks, TILE), F32),
            vmem((row_blocks, k_count, TILE), F32),
            vmem((row_blocks, k_count, TILE), F32),
            vmem((row_blocks, k_count, TILE), F32),
            vmem((wide_parts, tall_parts, blocks_here, width), F32),
            vmem((tall_parts, wide_parts - 1, blocks_here, width), F32),
            vmem((tall_parts - 1, blocks_here, width), F32),
            vmem((tall_parts - 1, blocks_here, width), F32),
            vmem((blocks_here, k_count, TILE), F32),
            dma((11,)),
            dma((chunks,)),
            dma((tall_parts - 1, pieces)),
            dma((tall_parts - 1, pieces)),
            dma((tall_parts, wide_parts - 1, pieces)),
            dma((tall_parts, wide_parts - 1, pieces)),
            dma((2,)),
            dma((2,)),
            dma((tall_parts, wide_parts - 1)),
            dma((tall_parts, wide_parts - 1)),
            dma((tall_parts - 1,)),
            dma((tall_parts - 1,)),
        ],
        compiler_params=pltpu.CompilerParams(
            collective_id=0, has_side_effects=True, vmem_limit_bytes=40 * 1024 * 1024
        ),
    )(*[x if x is tile_count else pltpu.with_memory_space_constraint(x, pltpu.HBM) for x in operands])


def solution(mesh):
    return jax.shard_map(
        local,
        mesh=mesh,
        in_specs=(
            P("plans", "beam", "vox"),
            P(("plans", "vox"), "beam", None, None, None),
            P(("plans", "vox"), "beam", None),
            P(("plans", "vox"), "beam", None),
            P(("plans", "vox"), "beam"),
            P(("plans", "vox")),
            P("plans"),
            P("plans", None),
            P("plans"),
            P("plans", None),
        ),
        out_specs=(P("plans", "vox"), P("plans", "beam", "vox")),
        check_vma=False,
    )
```

```python
import functools

import jax
import jax.numpy as jnp
from jax import lax
from jax.experimental import pallas as pl
from jax.experimental.pallas import tpu as pltpu
from jax.sharding import PartitionSpec as P

TILE = 128
BLB = 512
MESH = pl.DeviceIdType.MESH
F32 = jnp.float32
BF16 = jnp.bfloat16


def two_terms(x):
    high = x.astype(BF16)
    return high, (x - high.astype(F32)).astype(BF16)


def three_terms(x):
    high = x.astype(BF16)
    rest = x - high.astype(F32)
    middle = rest.astype(BF16)
    return high, middle, (rest - middle.astype(F32)).astype(BF16)


def dot(a, b, on=0):
    return lax.dot_general(a, b, (((1,), (on,)), ((), ())), preferred_element_type=F32)


def kernel(
    wide_parts,
    tall_parts,
    groups,
    fluence_in,
    values,
    row_in,
    column_in,
    count_in,
    labels_in,
    prescribed_in,
    weights_in,
    smoothing_in,
    neighbours_in,
    dose_out,
    gradient_out,
    fluence,
    row_list,
    column_list,
    row_vector,
    column_vector,
    count,
    labels,
    prescribed,
    weights,
    smoothing,
    neighbours,
    tiles,
    split,
    own,
    other,
    product,
    partial,
    partner_partial,
    target,
    scaled,
    residual,
    terms,
    beside_terms,
    middle_terms,
    far_terms,
    base,
    small_sem,
    load_sem,
    tall_send,
    tall_recv,
    wide_send,
    wide_recv,
    pair_send,
    pair_recv,
    first_send,
    first_recv,
    second_send,
    second_recv,
):
    me = lax.axis_index("vox")
    group = lax.axis_index("beam")
    partner = lax.rem(group + 1, groups)
    tall, wide = me // wide_parts, me % wide_parts
    k_count = fluence.shape[0]
    blocks_here = fluence.shape[2] // TILE
    row_blocks = labels.shape[0]
    slots = tiles.shape[0]
    column_blocks = own.shape[0]
    structures = prescribed.shape[0]
    chunks = load_sem.shape[0]
    chunk = slots // chunks
    tall_at = [lax.rem(tall + step, tall_parts) for step in range(tall_parts)]
    tall_from = [lax.rem(tall + tall_parts - step, tall_parts) for step in range(tall_parts)]
    tall_peers = [at * wide_parts + wide for at in tall_at]
    wide_peers = [
        tall * wide_parts + lax.rem(wide + step, wide_parts) for step in range(wide_parts)
    ]

    def remote(source, target_ref, send, recv, axis, peer):
        copy = pltpu.make_async_remote_copy(
            src_ref=source,
            dst_ref=target_ref,
            send_sem=send,
            recv_sem=recv,
            device_id={axis: peer},
            device_id_type=MESH,
        )
        copy.start()
        return copy

    barrier = pltpu.get_barrier_semaphore()
    for peer in tall_peers[1:] + wide_peers[1:]:
        pl.semaphore_signal(barrier, inc=1, device_id={"vox": peer}, device_id_type=MESH)
    pl.semaphore_signal(barrier, inc=1, device_id={"beam": partner}, device_id_type=MESH)

    small = []
    for index, (source, place) in enumerate(
        (
            (fluence_in, fluence),
            (labels_in, labels),
            (prescribed_in, prescribed),
            (weights_in, weights),
            (column_in, column_list),
            (column_in, column_vector),
            (row_in, row_list),
            (row_in, row_vector),
            (count_in, count),
            (smoothing_in, smoothing),
            (neighbours_in, neighbours),
        )
    ):
        copy = pltpu.make_async_copy(source, place, small_sem.at[index])
        copy.start()
        small.append(copy)
    loads = []
    for part in range(chunks):
        here = pl.ds(part * chunk, chunk)
        copy = pltpu.make_async_copy(values.at[0, 0, here], tiles.at[here], load_sem.at[part])
        copy.start()
        loads.append(copy)

    small[0].wait()
    for block in range(blocks_here):
        own[me * blocks_here + block] = fluence[:, 0, block * TILE : (block + 1) * TILE]

    pl.semaphore_wait(barrier, tall_parts + wide_parts - 1)

    def shard_of(part):
        return own.at[pl.ds(part * blocks_here, blocks_here)]

    def along_wide(step, part):
        return [
            remote(
                shard_of(part),
                shard_of(part),
                wide_send.at[step, near],
                wide_recv.at[step, near],
                "vox",
                wide_peers[near + 1],
            )
            for near in range(wide_parts - 1)
        ]

    tall_copies = [
        remote(
            shard_of(me),
            shard_of(me),
            tall_send.at[step - 1],
            tall_recv.at[step - 1],
            "vox",
            tall_peers[step],
        )
        for step in range(1, tall_parts)
    ]
    wide_copies = along_wide(0, me)

    def split_chunk(part):
        loads[part].wait()
        for slot in range(part * chunk, (part + 1) * chunk):
            high, low = two_terms(tiles[slot])
            split[slot, :TILE] = high
            split[slot, TILE:] = low

    for copy in small[1:]:
        copy.wait()
    k_index = lax.broadcasted_iota(jnp.int32, (k_count, TILE), 0)

    def spread_over_k(read):
        column = jnp.zeros((k_count, TILE), F32)
        for k in range(k_count):
            column = jnp.where(k_index == k, read(k), column)
        return column

    def structure_values():
        weight_of = [spread_over_k(lambda k, s=s: weights[s, k]) for s in range(structures)]
        for row in range(row_blocks):
            label = jnp.broadcast_to(labels[row : row + 1, :], (k_count, TILE))
            level = jnp.zeros((k_count, TILE), F32)
            factor = jnp.zeros((k_count, TILE), F32)
            for structure in range(structures):
                member = label == structure
                level = jnp.where(member, prescribed[structure], level)
                factor = jnp.where(member, weight_of[structure], factor)
            target[row] = level
            scaled[row] = factor

    for part in range(chunks // 2):
        split_chunk(part)
    work = [functools.partial(split_chunk, part) for part in range(chunks // 2, chunks)]
    work.append(structure_values)
    for step in range(1, tall_parts):
        tall_copies[step - 1].wait_recv()
        wide_copies += along_wide(step, tall_from[step] * wide_parts + wide)
        if work:
            work.pop(0)()
    for piece in work:
        piece()
    for copy in wide_copies:
        copy.wait_recv()

    share = remote(own, other, pair_send.at[0], pair_recv.at[0], "beam", partner)

    for slot in range(slots):
        high, low = two_terms(own[column_list[0, 0, slot]])
        out = dot(jnp.concatenate([high, low], axis=0), split[slot], on=1)
        out = out[:k_count] + out[k_count:]
        product[pl.ds(slot, k_count, stride=slots), :] = out[:, :TILE] + out[:, TILE:]

    active = lax.broadcasted_iota(jnp.int32, (1, slots), 1) < count[0, 0]

    def products():
        return three_terms(
            jnp.concatenate(
                [product[k * slots : (k + 1) * slots, :] for k in range(k_count)], axis=1
            )
        )

    def placed(vector, blocks, three):
        place = jnp.where((vector == blocks) & active, 1.0, 0.0).astype(BF16)
        high, middle, low = three
        return dot(place, high) + (dot(place, middle) + dot(place, low))

    dose = placed(
        row_vector[0], lax.broadcasted_iota(jnp.int32, (row_blocks, slots), 0), products()
    )
    for k in range(k_count):
        partial[k * row_blocks : (k + 1) * row_blocks, :] = dose[:, k * TILE : (k + 1) * TILE]
    swap = remote(partial, partner_partial, pair_send.at[1], pair_recv.at[1], "beam", partner)
    swap.wait_recv()
    for row in range(row_blocks):
        where = pl.ds(row, k_count, stride=row_blocks)
        total = partial[where, :] + partner_partial[where, :]
        dose_out[:, row * TILE : (row + 1) * TILE] = total
        label = jnp.broadcast_to(labels[row : row + 1, :], (k_count, TILE))
        excess = total - target[row]
        excess = jnp.where(label == 0, excess, jnp.maximum(excess, 0.0))
        residual[row] = scaled[row] * excess

    for slot in range(slots):
        high, low = two_terms(residual[row_list[0, 0, slot]])
        both = jnp.concatenate([high, low], axis=0)
        out = dot(jnp.concatenate([both, both], axis=1), split[slot])
        product[pl.ds(slot, k_count, stride=slots), :] = out[:k_count] + out[k_count:]

    three = products()
    line = lax.broadcasted_iota(jnp.int32, (tall_parts * blocks_here, slots), 0)
    line_tall, line_block = line // blocks_here, line % blocks_here

    def make_terms(near):
        at = lax.rem(wide + near, wide_parts)
        found = placed(column_vector[0], (line_tall * wide_parts + at) * blocks_here + line_block, three)
        for part in range(tall_parts):
            terms[near, part] = found[part * blocks_here : (part + 1) * blocks_here, :]

    steps = list(range(1, tall_parts)) + [0]
    halves = [pl.ds(half * (k_count // 2) * TILE, k_count // 2 * TILE) for half in range(2)]
    first_copies = {(step, half): [] for step in steps for half in range(2)}
    for near in range(1, wide_parts):
        make_terms(near)
        for half, lanes in enumerate(halves):
            for step in steps:
                first_copies[step, half].append(
                    remote(
                        terms.at[near, tall_at[step], :, lanes],
                        beside_terms.at[step, near - 1, :, lanes],
                        first_send.at[step, near - 1, half],
                        first_recv.at[step, near - 1, half],
                        "vox",
                        wide_peers[near],
                    )
                )
    make_terms(0)

    def gathered(step, half):
        total = terms[0, tall_at[step], :, halves[half]]
        for near, copy in enumerate(first_copies[step, half]):
            copy.wait_recv()
            total = total + beside_terms[step, near, :, halves[half]]
        return total

    second_copies = []
    for half, lanes in enumerate(halves):
        for step in range(1, tall_parts):
            middle_terms[step - 1, :, lanes] = gathered(step, half)
            second_copies.append(
                remote(
                    middle_terms.at[step - 1, :, lanes],
                    far_terms.at[step - 1, :, lanes],
                    second_send.at[step - 1, half],
                    second_recv.at[step - 1, half],
                    "vox",
                    tall_peers[step],
                )
            )

    share.wait_recv()
    smooth = spread_over_k(lambda k: smoothing[k])
    per_beam = BLB // TILE
    group_beams = column_blocks // per_beam
    near_count = neighbours.shape[0]
    for block in range(blocks_here):
        place = group * column_blocks + me * blocks_here + block
        beam = place // per_beam
        within = place % per_beam
        around = jnp.zeros((k_count, TILE), F32)
        for n in range(near_count):
            beside = neighbours[n, beam]
            beside_group = jnp.where(beside >= group_beams, 1, 0)
            at = (beside - beside_group * group_beams) * per_beam + within
            around = around + jnp.where(beside_group == group, own[at], other[at])
        here = fluence[:, 0, block * TILE : (block + 1) * TILE]
        base[block] = smooth * (near_count * here - around)

    swap.wait_send()
    total = jnp.concatenate([gathered(0, 0), gathered(0, 1)], axis=1)
    for copy in second_copies:
        copy.wait_recv()
    for step in range(1, tall_parts):
        total = total + far_terms[step - 1]
    for k in range(k_count):
        partial[k * blocks_here : (k + 1) * blocks_here, :] = total[:, k * TILE : (k + 1) * TILE]
    for block in range(blocks_here):
        summed = partial[pl.ds(block, k_count, stride=blocks_here), :]
        gradient_out[:, 0, block * TILE : (block + 1) * TILE] = summed + base[block]

    for copy in tall_copies + wide_copies + second_copies + [share]:
        copy.wait_send()
    for copies in first_copies.values():
        for copy in copies:
            copy.wait_send()


def local(
    fluence,
    tile_values,
    tile_rows,
    tile_columns,
    tile_count,
    labels,
    prescribed,
    weights,
    smoothing,
    beam_neighbours,
):
    groups = lax.axis_size("beam")
    parts = lax.axis_size("vox")
    wide_parts = max(w for w in range(1, parts + 1) if parts % w == 0 and w * w <= parts)
    tall_parts = parts // wide_parts
    k_count, _, shard = fluence.shape
    blocks_here = shard // TILE
    column_blocks = blocks_here * parts
    row_blocks = labels.shape[0] // TILE
    slots = tile_values.shape[2]
    chunks = 4
    width = k_count * TILE
    operands = (
        fluence,
        tile_values,
        tile_rows,
        tile_columns,
        tile_count,
        labels.reshape(row_blocks, TILE),
        prescribed,
        weights.T,
        smoothing,
        beam_neighbours.T,
    )

    def on_chip(array, space):
        return space(array.shape, array.dtype)

    vmem, smem = pltpu.VMEM, pltpu.SMEM
    dma = pltpu.SemaphoreType.DMA
    out = pl.BlockSpec(memory_space=pltpu.VMEM)
    return pl.pallas_call(
        functools.partial(kernel, wide_parts, tall_parts, groups),
        out_shape=(
            jax.ShapeDtypeStruct((k_count, row_blocks * TILE), F32),
            jax.ShapeDtypeStruct(fluence.shape, F32),
        ),
        in_specs=[pl.BlockSpec(memory_space=pltpu.HBM)] * len(operands),
        out_specs=(out, out),
        scratch_shapes=[
            on_chip(fluence, vmem),
            on_chip(tile_rows, smem),
            on_chip(tile_columns, smem),
            on_chip(tile_rows, vmem),
            on_chip(tile_columns, vmem),
            on_chip(tile_count, smem),
            on_chip(operands[5], vmem),
            on_chip(prescribed, smem),
            on_chip(operands[7], smem),
            on_chip(smoothing, smem),
            on_chip(operands[9], smem),
            vmem((slots, TILE, TILE), F32),
            vmem((slots, 2 * TILE, TILE), BF16),
            vmem((column_blocks, k_count, TILE), F32),
            vmem((column_blocks, k_count, TILE), F32),
            vmem((k_count * slots, TILE), F32),
            vmem((k_count * row_blocks, TILE), F32),
            vmem((k_count * row_blocks, TILE), F32),
            vmem((row_blocks, k_count, TILE), F32),
            vmem((row_blocks, k_count, TILE), F32),
            vmem((row_blocks, k_count, TILE), F32),
            vmem((wide_parts, tall_parts, blocks_here, width), F32),
            vmem((tall_parts, wide_parts - 1, blocks_here, width), F32),
            vmem((tall_parts - 1, blocks_here, width), F32),
            vmem((tall_parts - 1, blocks_here, width), F32),
            vmem((blocks_here, k_count, TILE), F32),
            dma((11,)),
            dma((chunks,)),
            dma((tall_parts - 1,)),
            dma((tall_parts - 1,)),
            dma((tall_parts, wide_parts - 1)),
            dma((tall_parts, wide_parts - 1)),
            dma((2,)),
            dma((2,)),
            dma((tall_parts, wide_parts - 1, 2)),
            dma((tall_parts, wide_parts - 1, 2)),
            dma((tall_parts - 1, 2)),
            dma((tall_parts - 1, 2)),
        ],
        compiler_params=pltpu.CompilerParams(
            collective_id=0, has_side_effects=True, vmem_limit_bytes=40 * 1024 * 1024
        ),
    )(*[x if x is tile_count else pltpu.with_memory_space_constraint(x, pltpu.HBM) for x in operands])


def solution(mesh):
    return jax.shard_map(
        local,
        mesh=mesh,
        in_specs=(
            P("plans", "beam", "vox"),
            P(("plans", "vox"), "beam", None, None, None),
            P(("plans", "vox"), "beam", None),
            P(("plans", "vox"), "beam", None),
            P(("plans", "vox"), "beam"),
            P(("plans", "vox")),
            P("plans"),
            P("plans", None),
            P("plans"),
            P("plans", None),
        ),
        out_specs=(P("plans", "vox"), P("plans", "beam", "vox")),
        check_vma=False,
    )
```

```python
import functools

import jax
import jax.numpy as jnp
from jax import lax
from jax.experimental import pallas as pl
from jax.experimental.pallas import tpu as pltpu
from jax.sharding import PartitionSpec as P

TILE = 128
BLB = 512
MESH = pl.DeviceIdType.MESH
F32 = jnp.float32
BF16 = jnp.bfloat16


def two_terms(x):
    high = x.astype(BF16)
    return high, (x - high.astype(F32)).astype(BF16)


def three_terms(x):
    high = x.astype(BF16)
    rest = x - high.astype(F32)
    middle = rest.astype(BF16)
    return high, middle, (rest - middle.astype(F32)).astype(BF16)


def dot(a, b, on=0):
    return lax.dot_general(a, b, (((1,), (on,)), ((), ())), preferred_element_type=F32)


def kernel(
    wide_parts,
    tall_parts,
    groups,
    fluence_in,
    values,
    row_in,
    column_in,
    count_in,
    labels_in,
    prescribed_in,
    weights_in,
    smoothing_in,
    neighbours_in,
    dose_out,
    gradient_out,
    fluence,
    row_list,
    column_list,
    row_vector,
    column_vector,
    count,
    labels,
    prescribed,
    weights,
    smoothing,
    neighbours,
    tiles,
    split,
    own,
    other,
    product,
    partial,
    partner_partial,
    target,
    scaled,
    residual,
    terms,
    beside_terms,
    middle_terms,
    far_terms,
    base,
    small_sem,
    load_sem,
    tall_send,
    tall_recv,
    wide_send,
    wide_recv,
    pair_send,
    pair_recv,
    first_send,
    first_recv,
    second_send,
    second_recv,
):
    me = lax.axis_index("vox")
    group = lax.axis_index("beam")
    partner = lax.rem(group + 1, groups)
    tall, wide = me // wide_parts, me % wide_parts
    k_count = fluence.shape[0]
    blocks_here = fluence.shape[2] // TILE
    row_blocks = labels.shape[0]
    slots = tiles.shape[0]
    column_blocks = own.shape[0]
    structures = prescribed.shape[0]
    chunks = load_sem.shape[0]
    chunk = slots // chunks
    tall_at = [lax.rem(tall + step, tall_parts) for step in range(tall_parts)]
    tall_from = [lax.rem(tall + tall_parts - step, tall_parts) for step in range(tall_parts)]
    tall_peers = [at * wide_parts + wide for at in tall_at]
    wide_peers = [
        tall * wide_parts + lax.rem(wide + step, wide_parts) for step in range(wide_parts)
    ]

    def remote(source, target_ref, send, recv, axis, peer):
        copy = pltpu.make_async_remote_copy(
            src_ref=source,
            dst_ref=target_ref,
            send_sem=send,
            recv_sem=recv,
            device_id={axis: peer},
            device_id_type=MESH,
        )
        copy.start()
        return copy

    barrier = pltpu.get_barrier_semaphore()
    for peer in tall_peers[1:] + wide_peers[1:]:
        pl.semaphore_signal(barrier, inc=1, device_id={"vox": peer}, device_id_type=MESH)
    pl.semaphore_signal(barrier, inc=1, device_id={"beam": partner}, device_id_type=MESH)

    small = []
    for index, (source, place) in enumerate(
        (
            (fluence_in, fluence),
            (labels_in, labels),
            (prescribed_in, prescribed),
            (weights_in, weights),
            (column_in, column_list),
            (column_in, column_vector),
            (row_in, row_list),
            (row_in, row_vector),
            (count_in, count),
            (smoothing_in, smoothing),
            (neighbours_in, neighbours),
        )
    ):
        copy = pltpu.make_async_copy(source, place, small_sem.at[index])
        copy.start()
        small.append(copy)
    loads = []
    for part in range(chunks):
        here = pl.ds(part * chunk, chunk)
        copy = pltpu.make_async_copy(values.at[0, 0, here], tiles.at[here], load_sem.at[part])
        copy.start()
        loads.append(copy)

    small[0].wait()
    for block in range(blocks_here):
        own[me * blocks_here + block] = fluence[:, 0, block * TILE : (block + 1) * TILE]

    pl.semaphore_wait(barrier, tall_parts + wide_parts - 1)

    def shard_of(part):
        return own.at[pl.ds(part * blocks_here, blocks_here)]

    def along_wide(step, part):
        return [
            remote(
                shard_of(part),
                shard_of(part),
                wide_send.at[step, near],
                wide_recv.at[step, near],
                "vox",
                wide_peers[near + 1],
            )
            for near in range(wide_parts - 1)
        ]

    tall_copies = [
        remote(
            shard_of(me),
            shard_of(me),
            tall_send.at[step - 1],
            tall_recv.at[step - 1],
            "vox",
            tall_peers[step],
        )
        for step in range(1, tall_parts)
    ]
    wide_copies = along_wide(0, me)

    def split_chunk(part):
        loads[part].wait()
        for slot in range(part * chunk, (part + 1) * chunk):
            high, low = two_terms(tiles[slot])
            split[slot, :TILE] = high
            split[slot, TILE:] = low

    for copy in small[1:]:
        copy.wait()
    k_index = lax.broadcasted_iota(jnp.int32, (k_count, TILE), 0)

    def spread_over_k(read):
        column = jnp.zeros((k_count, TILE), F32)
        for k in range(k_count):
            column = jnp.where(k_index == k, read(k), column)
        return column

    def structure_values():
        weight_of = [spread_over_k(lambda k, s=s: weights[s, k]) for s in range(structures)]
        for row in range(row_blocks):
            label = jnp.broadcast_to(labels[row : row + 1, :], (k_count, TILE))
            level = jnp.zeros((k_count, TILE), F32)
            factor = jnp.zeros((k_count, TILE), F32)
            for structure in range(structures):
                member = label == structure
                level = jnp.where(member, prescribed[structure], level)
                factor = jnp.where(member, weight_of[structure], factor)
            target[row] = level
            scaled[row] = factor

    for part in range(chunks // 2):
        split_chunk(part)
    work = [functools.partial(split_chunk, part) for part in range(chunks // 2, chunks)]
    work.append(structure_values)
    for step in range(1, tall_parts):
        tall_copies[step - 1].wait_recv()
        wide_copies += along_wide(step, tall_from[step] * wide_parts + wide)
        if work:
            work.pop(0)()
    for piece in work:
        piece()
    for copy in wide_copies:
        copy.wait_recv()

    share = remote(own, other, pair_send.at[0], pair_recv.at[0], "beam", partner)

    for slot in range(slots):
        high, low = two_terms(own[column_list[0, 0, slot]])
        out = dot(jnp.concatenate([high, low], axis=0), split[slot], on=1)
        out = out[:k_count] + out[k_count:]
        product[pl.ds(slot, k_count, stride=slots), :] = out[:, :TILE] + out[:, TILE:]

    active = lax.broadcasted_iota(jnp.int32, (1, slots), 1) < count[0, 0]

    def products():
        return three_terms(
            jnp.concatenate(
                [product[k * slots : (k + 1) * slots, :] for k in range(k_count)], axis=1
            )
        )

    def placed(vector, blocks, three):
        place = jnp.where((vector == blocks) & active, 1.0, 0.0).astype(BF16)
        high, middle, low = three
        return dot(place, high) + (dot(place, middle) + dot(place, low))

    dose = placed(
        row_vector[0], lax.broadcasted_iota(jnp.int32, (row_blocks, slots), 0), products()
    )
    for k in range(k_count):
        partial[k * row_blocks : (k + 1) * row_blocks, :] = dose[:, k * TILE : (k + 1) * TILE]
    swap = remote(partial, partner_partial, pair_send.at[1], pair_recv.at[1], "beam", partner)
    swap.wait_recv()
    for row in range(row_blocks):
        where = pl.ds(row, k_count, stride=row_blocks)
        total = partial[where, :] + partner_partial[where, :]
        dose_out[:, row * TILE : (row + 1) * TILE] = total
        label = jnp.broadcast_to(labels[row : row + 1, :], (k_count, TILE))
        excess = total - target[row]
        excess = jnp.where(label == 0, excess, jnp.maximum(excess, 0.0))
        residual[row] = scaled[row] * excess

    for slot in range(slots):
        high, low = two_terms(residual[row_list[0, 0, slot]])
        both = jnp.concatenate([high, low], axis=0)
        out = dot(jnp.concatenate([both, both], axis=1), split[slot])
        product[pl.ds(slot, k_count, stride=slots), :] = out[:k_count] + out[k_count:]

    three = products()
    line = lax.broadcasted_iota(jnp.int32, (tall_parts * blocks_here, slots), 0)
    line_tall, line_block = line // blocks_here, line % blocks_here

    def make_terms(near):
        at = lax.rem(wide + near, wide_parts)
        found = placed(column_vector[0], (line_tall * wide_parts + at) * blocks_here + line_block, three)
        for part in range(tall_parts):
            terms[near, part] = found[part * blocks_here : (part + 1) * blocks_here, :]

    steps = list(range(1, tall_parts)) + [0]
    halves = [pl.ds(half * (k_count // 4) * TILE, k_count // 4 * TILE) for half in range(4)]
    first_copies = {(step, half): [] for step in steps for half in range(4)}
    for near in range(1, wide_parts):
        make_terms(near)
        for half, lanes in enumerate(halves):
            for step in steps:
                first_copies[step, half].append(
                    remote(
                        terms.at[near, tall_at[step], :, lanes],
                        beside_terms.at[step, near - 1, :, lanes],
                        first_send.at[step, near - 1, half],
                        first_recv.at[step, near - 1, half],
                        "vox",
                        wide_peers[near],
                    )
                )
    make_terms(0)

    def gathered(step, half):
        total = terms[0, tall_at[step], :, halves[half]]
        for near, copy in enumerate(first_copies[step, half]):
            copy.wait_recv()
            total = total + beside_terms[step, near, :, halves[half]]
        return total

    second_copies = []
    for half, lanes in enumerate(halves):
        for step in range(1, tall_parts):
            middle_terms[step - 1, :, lanes] = gathered(step, half)
            second_copies.append(
                remote(
                    middle_terms.at[step - 1, :, lanes],
                    far_terms.at[step - 1, :, lanes],
                    second_send.at[step - 1, half],
                    second_recv.at[step - 1, half],
                    "vox",
                    tall_peers[step],
                )
            )

    share.wait_recv()
    smooth = spread_over_k(lambda k: smoothing[k])
    per_beam = BLB // TILE
    group_beams = column_blocks // per_beam
    near_count = neighbours.shape[0]
    for block in range(blocks_here):
        place = group * column_blocks + me * blocks_here + block
        beam = place // per_beam
        within = place % per_beam
        around = jnp.zeros((k_count, TILE), F32)
        for n in range(near_count):
            beside = neighbours[n, beam]
            beside_group = jnp.where(beside >= group_beams, 1, 0)
            at = (beside - beside_group * group_beams) * per_beam + within
            around = around + jnp.where(beside_group == group, own[at], other[at])
        here = fluence[:, 0, block * TILE : (block + 1) * TILE]
        base[block] = smooth * (near_count * here - around)

    swap.wait_send()
    total = jnp.concatenate([gathered(0, half) for half in range(4)], axis=1)
    for copy in second_copies:
        copy.wait_recv()
    for step in range(1, tall_parts):
        total = total + far_terms[step - 1]
    for k in range(k_count):
        partial[k * blocks_here : (k + 1) * blocks_here, :] = total[:, k * TILE : (k + 1) * TILE]
    for block in range(blocks_here):
        summed = partial[pl.ds(block, k_count, stride=blocks_here), :]
        gradient_out[:, 0, block * TILE : (block + 1) * TILE] = summed + base[block]

    for copy in tall_copies + wide_copies + second_copies + [share]:
        copy.wait_send()
    for copies in first_copies.values():
        for copy in copies:
            copy.wait_send()


def local(
    fluence,
    tile_values,
    tile_rows,
    tile_columns,
    tile_count,
    labels,
    prescribed,
    weights,
    smoothing,
    beam_neighbours,
):
    groups = lax.axis_size("beam")
    parts = lax.axis_size("vox")
    wide_parts = max(w for w in range(1, parts + 1) if parts % w == 0 and w * w <= parts)
    tall_parts = parts // wide_parts
    k_count, _, shard = fluence.shape
    blocks_here = shard // TILE
    column_blocks = blocks_here * parts
    row_blocks = labels.shape[0] // TILE
    slots = tile_values.shape[2]
    chunks = 4
    width = k_count * TILE
    operands = (
        fluence,
        tile_values,
        tile_rows,
        tile_columns,
        tile_count,
        labels.reshape(row_blocks, TILE),
        prescribed,
        weights.T,
        smoothing,
        beam_neighbours.T,
    )

    def on_chip(array, space):
        return space(array.shape, array.dtype)

    vmem, smem = pltpu.VMEM, pltpu.SMEM
    dma = pltpu.SemaphoreType.DMA
    out = pl.BlockSpec(memory_space=pltpu.VMEM)
    return pl.pallas_call(
        functools.partial(kernel, wide_parts, tall_parts, groups),
        out_shape=(
            jax.ShapeDtypeStruct((k_count, row_blocks * TILE), F32),
            jax.ShapeDtypeStruct(fluence.shape, F32),
        ),
        in_specs=[pl.BlockSpec(memory_space=pltpu.HBM)] * len(operands),
        out_specs=(out, out),
        scratch_shapes=[
            on_chip(fluence, vmem),
            on_chip(tile_rows, smem),
            on_chip(tile_columns, smem),
            on_chip(tile_rows, vmem),
            on_chip(tile_columns, vmem),
            on_chip(tile_count, smem),
            on_chip(operands[5], vmem),
            on_chip(prescribed, smem),
            on_chip(operands[7], smem),
            on_chip(smoothing, smem),
            on_chip(operands[9], smem),
            vmem((slots, TILE, TILE), F32),
            vmem((slots, 2 * TILE, TILE), BF16),
            vmem((column_blocks, k_count, TILE), F32),
            vmem((column_blocks, k_count, TILE), F32),
            vmem((k_count * slots, TILE), F32),
            vmem((k_count * row_blocks, TILE), F32),
            vmem((k_count * row_blocks, TILE), F32),
            vmem((row_blocks, k_count, TILE), F32),
            vmem((row_blocks, k_count, TILE), F32),
            vmem((row_blocks, k_count, TILE), F32),
            vmem((wide_parts, tall_parts, blocks_here, width), F32),
            vmem((tall_parts, wide_parts - 1, blocks_here, width), F32),
            vmem((tall_parts - 1, blocks_here, width), F32),
            vmem((tall_parts - 1, blocks_here, width), F32),
            vmem((blocks_here, k_count, TILE), F32),
            dma((11,)),
            dma((chunks,)),
            dma((tall_parts - 1,)),
            dma((tall_parts - 1,)),
            dma((tall_parts, wide_parts - 1)),
            dma((tall_parts, wide_parts - 1)),
            dma((2,)),
            dma((2,)),
            dma((tall_parts, wide_parts - 1, 4)),
            dma((tall_parts, wide_parts - 1, 4)),
            dma((tall_parts - 1, 4)),
            dma((tall_parts - 1, 4)),
        ],
        compiler_params=pltpu.CompilerParams(
            collective_id=0, has_side_effects=True, vmem_limit_bytes=40 * 1024 * 1024
        ),
    )(*[x if x is tile_count else pltpu.with_memory_space_constraint(x, pltpu.HBM) for x in operands])


def solution(mesh):
    return jax.shard_map(
        local,
        mesh=mesh,
        in_specs=(
            P("plans", "beam", "vox"),
            P(("plans", "vox"), "beam", None, None, None),
            P(("plans", "vox"), "beam", None),
            P(("plans", "vox"), "beam", None),
            P(("plans", "vox"), "beam"),
            P(("plans", "vox")),
            P("plans"),
            P("plans", None),
            P("plans"),
            P("plans", None),
        ),
        out_specs=(P("plans", "vox"), P("plans", "beam", "vox")),
        check_vma=False,
    )
```
